32 devices in a mesh: row: 8 (over z, y), col: 4 (over x, core).
Axes of the slice: x: 2, y: 2, z: 4, core: 2. Of those that a mesh axis runs over, the one named last changes fastest.
Arguments:
- similarity: bfloat16 [4096, 4096], P('row', 'col'), may hold values from 0.0009 to 1
- occupancy: int32 [32, 32], P('row', 'col'), may hold values from 0 to 1, as said below
- kept_tiles: int32 [32, 32], P('row', 'col'), may hold values from 0 to 1, as said below
Outputs:
- flow: bfloat16 [4096, 4096], P('row', 'col')
The draws below stay inside these ranges and needn't reach their ends.
Inputs may be any that keep to these rules, and one draw needn't show every extreme that they name: `occupancy`: 0 or 1; every diagonal tile is 1; the share of ones varies from tile row to tile row. `kept_tiles`: 0 or 1; every diagonal tile is 1; the share of ones varies from tile row to tile row.
All inputs are finite; a program needn't handle non-finite values.
Results may differ from the reference program's by a relative error of at most 0.001.
Values may be sent and summed in bfloat16 or wider, within the bound.
A program may use at most 64 MiB of HBM per device.

```python
import jax
import jax.numpy as jnp
from jax import lax

TILE = 128
NT = 32
N = 4096


def tile_draw(key, salt):
    first, second = jax.random.split(jax.random.fold_in(key, salt))
    level = jax.random.randint(first, (NT, 1), 20, 95)
    rolls = jax.random.randint(second, (NT, NT), 0, 100)
    picked = (rolls < level).astype(jnp.int32)
    diagonal = lax.broadcasted_iota(jnp.int32, (NT, NT), 0) == lax.broadcasted_iota(jnp.int32, (NT, NT), 1)
    return jnp.where(diagonal, 1, picked).astype(jnp.int32)


def draw_occupancy(key, part):
    return tile_draw(key, 11)


def draw_kept_tiles(key, part):
    return tile_draw(key, 23)


def draw_similarity(key, part):
    base_key, pick_key, value_key = jax.random.split(jax.random.fold_in(key, 37), 3)
    weak = jax.random.uniform(base_key, (N, N), jnp.float32, 0.001, 0.005)
    rolls = jax.random.uniform(pick_key, (N, N), jnp.float32, 0.0, 1.0)
    strong = jnp.exp(jax.random.uniform(value_key, (N, N), jnp.float32, jnp.log(0.1), 0.0))
    chosen = rolls < 0.06
    return jnp.where(chosen, strong, weak).astype(jnp.bfloat16)


def setup_inputs(seed: int = 0) -> dict:
    key_of = jax.random.split(jax.random.key(seed), 4)
    return {
        "similarity": draw_similarity(jax.random.fold_in(key_of[3], 71), 0),
        "occupancy": draw_occupancy(jax.random.fold_in(key_of[3], 71), 0),
        "kept_tiles": draw_kept_tiles(jax.random.fold_in(key_of[3], 71), 0),
    }


def expand_tiles(values, tile_pattern, tile_size):
    rows, cols = values.shape
    shaped = values.reshape(rows // tile_size, tile_size, cols // tile_size, tile_size)
    masked = shaped * tile_pattern.astype(values.dtype)[:, None, :, None]
    return masked.reshape(rows, cols)


def reference(similarity, occupancy, kept_tiles):
    stored = expand_tiles(similarity, occupancy, TILE)
    wide = stored.astype(jnp.float32)
    expanded = jnp.dot(wide, wide, preferred_element_type=jnp.float32)
    inflated = expand_tiles(expanded * expanded, kept_tiles, TILE)
    column_total = jnp.sum(inflated, axis=0)
    return (N * inflated / column_total[None, :]).astype(jnp.bfloat16)
```

```python
import functools

import jax
import jax.numpy as jnp
from jax import lax
from jax.experimental import pallas as pl
from jax.experimental.pallas import tpu as pltpu
from jax.sharding import PartitionSpec as P

TILE = 128
MESH = pl.DeviceIdType.MESH


def kernel(
    nz, nx, nq, order,
    sim, occ, kept, out,
    rp, cp, acc, obuf, tsend, trecv, ksend, kbuf,
    z_send, z_recv, pa_send, pa_recv, yc_send, yc_recv, yf_send, yf_recv,
    yb_send, yb_recv, xo_send, xo_recv, xf_send, xf_recv, xd_send, xd_recv, xg_send, xg_recv,
    t_send, t_recv, o_send, o_recv, k_send, k_recv,
):
    R, W = sim.shape
    H = W // 2
    CW = H // nq
    ir, ic = lax.axis_index("row"), lax.axis_index("col")
    z, y = lax.div(ir, 2), lax.rem(ir, 2)
    x, c = lax.div(ic, 2), lax.rem(ic, 2)
    oy, oc = 1 - y, 1 - c
    home = c == y

    def dev(xx, yy, zz, cc):
        return (zz * 2 + yy, xx * 2 + cc)

    def mult(v, m):
        return pl.multiple_of(v, m)

    def rows(yy):
        return pl.ds(mult(yy * R, R), R)

    def cols(start, width):
        return pl.ds(mult(start, TILE), width)

    def remote(src, dst, ssem, rsem, to):
        return pltpu.make_async_remote_copy(
            src_ref=src, dst_ref=dst, send_sem=ssem, recv_sem=rsem, device_id=to, device_id_type=MESH
        )

    partner = dev(x, y, z, oc)
    across = dev(x, oy, z, c)
    started = []

    def go(copy, cond=None):
        if cond is None:
            copy.start()
        else:
            pl.when(cond)(copy.start)
        started.append((copy, cond))

    barrier = pltpu.get_barrier_semaphore()
    peers = [partner, across, dev(x, oy, z, oc)]
    peers += [dev(lax.rem(x + d, nx), y, z, c) for d in range(1, nx)]
    peers += [dev(x, y, lax.rem(z + d, nz), c) for d in range(1, nz)]
    for peer in peers:
        pl.semaphore_signal(barrier, inc=1, device_id=peer, device_id_type=MESH)

    mycol = (2 * x + c) * W
    for i in range(R // TILE):
        for j in range(W // TILE):
            flag = occ[i, j].astype(jnp.float32)
            tile = sim[i * TILE : (i + 1) * TILE, j * TILE : (j + 1) * TILE].astype(jnp.float32)
            rp[pl.ds(mult(y * R + i * TILE, TILE), TILE), cols(mycol + j * TILE, TILE)] = (tile * flag).astype(
                jnp.bfloat16
            )
    ksend[...] = jnp.zeros_like(ksend)
    for i in range(R // TILE):
        for j in range(W // TILE):
            ksend[i : i + 1, j * TILE : (j + 1) * TILE] = jnp.full(
                (1, TILE), kept[i, j].astype(jnp.float32), jnp.float32
            )
    pl.semaphore_wait(barrier, len(peers))

    mine = rp.at[rows(y), cols(mycol, W)]

    def half_of(yy, start, hh):
        return rp.at[rows(yy), cols(start + hh * H, H)]

    for j, hh in enumerate((oc, c)):
        ref = half_of(y, mycol, hh)
        go(remote(ref, ref, pa_send.at[j], pa_recv.at[j], partner))

    def pa_arrive(j):
        ref = half_of(y, (2 * x + oc) * W, c if j == 0 else oc)
        remote(ref, ref, pa_send.at[j], pa_recv.at[j], partner).wait_recv()

    def piece(yy, core, q, hh):
        return rp.at[rows(yy), cols((2 * x + core) * W + hh * H + q * CW, CW)]

    for q in range(nq):
        for j, hh in enumerate((oc, c)):
            ref = piece(y, c, q, hh)
            go(remote(ref, ref, yc_send.at[q, j], yc_recv.at[q, j], across), jnp.logical_not(home))

    for d in range(1, nx):
        to = dev(lax.rem(x + d, nx), y, z, c)
        go(remote(mine, mine, xo_send.at[d], xo_recv.at[d], to))

    for hh in range(2):
        src = ksend.at[:, pl.ds(hh * H, H)]
        here = jnp.logical_and(home, c == hh)
        go(
            remote(src, kbuf.at[y], k_send.at[hh], k_recv.at[y], dev(x, c, z, hh)),
            jnp.logical_not(here),
        )

        @pl.when(here)
        def _():
            pltpu.make_async_copy(src, kbuf.at[y], k_recv.at[y]).start()

    tcol = (2 * x + y) * W + c * H

    def yy_of(h):
        return y if h == 0 else oy

    def own_part(q, h):
        return rp.at[rows(yy_of(h)), cols(tcol + q * CW, CW)]

    def slot(zb, q, h):
        return cp.at[zb, rows(yy_of(h)), pl.ds(q * CW, CW)]

    def own_sends(q, h):
        go(
            remote(own_part(q, h), slot(z, q, h), z_send.at[0, z, q, h], z_recv.at[z, q, h], dev(x, y, lax.rem(z + 1, nz), c)),
            z < nz - 1,
        )
        go(
            remote(own_part(q, h), slot(z, q, h), z_send.at[1, z, q, h], z_recv.at[z, q, h], dev(x, y, lax.rem(z + nz - 1, nz), c)),
            z > 0,
        )

    def arrivals(d, q, up):
        zb = lax.rem(z + nz - d, nz) if up else lax.rem(z + d, nz)
        valid = z >= d if up else z + d < nz
        onward = jnp.logical_and(valid, z < nz - 1) if up else jnp.logical_and(valid, z > 0)
        nxt = lax.rem(z + 1, nz) if up else lax.rem(z + nz - 1, nz)
        side = 0 if up else 1
        for h in range(2):
            ref = slot(zb, q, h)
            copy = remote(ref, ref, z_send.at[side, zb, q, h], z_recv.at[zb, q, h], dev(x, y, nxt, c))
            pl.when(valid)(copy.wait_recv)
            go(copy, onward)

    def y_pieces(q):
        for j, hh in enumerate((oc, c)):
            ref = piece(oy, c, q, hh)
            pl.when(home)(remote(ref, ref, yc_send.at[q, j], yc_recv.at[q, j], across).wait_recv)
            go(remote(ref, ref, yf_send.at[q, j], yf_recv.at[q, j], partner), home)

    def y_passed(q, j):
        ref = piece(oy, oc, q, c if j == 0 else oc)
        pl.when(jnp.logical_not(home))(
            remote(ref, ref, yf_send.at[q, j], yf_recv.at[q, j], partner).wait_recv
        )

    ycol_ref = rp.at[rows(oy), cols(mycol, W)]

    def pass_x(cond):
        for d in range(1, nx):
            to = dev(lax.rem(x + d, nx), y, z, c)
            go(remote(ycol_ref, ycol_ref, xd_send.at[d], xd_recv.at[d], to), cond)

    def x_arrive(recv, send, recv2, send2, yy):
        for d in range(1, nx):
            src_x = lax.rem(x + nx - d, nx)
            ref = rp.at[rows(yy), cols((2 * src_x + c) * W, W)]
            remote(ref, ref, send.at[d], recv.at[d], partner).wait_recv()
            go(remote(ref, ref, send2.at[d], recv2.at[d], partner))

    def x_passed(recv2, send2, yy):
        for d in range(1, nx):
            src_x = lax.rem(x + nx - d, nx)
            ref = rp.at[rows(yy), cols((2 * src_x + oc) * W, W)]
            remote(ref, ref, send2.at[d], recv2.at[d], partner).wait_recv()

    low = z < (nz + 1) // 2

    def zb_of(d):
        return jnp.where(low, lax.rem(z + d, nz), lax.rem(z + nz - d, nz))

    def multiply(q, ds):
        for h in range(2):
            part = None
            for d in ds:
                zb = zb_of(d) if d else z
                lhs = rp[pl.ds(h * R, R), pl.ds(mult(zb * 2 * R, 2 * R), 2 * R)]
                if d:
                    rhs = cp[zb, :, pl.ds(q * CW, CW)]
                else:
                    rhs = rp[:, cols(tcol + q * CW, CW)]
                prod = jnp.dot(lhs, rhs, preferred_element_type=jnp.float32)
                part = prod if part is None else part + prod
            where = (pl.ds(h * R, R), pl.ds(q * CW, CW))
            if ds[0]:
                acc[where] = acc[where] + part
            else:
                acc[where] = part

    def inflate(q):
        total = jnp.zeros((1, CW), jnp.float32)
        for h in range(2):
            for i in range(R // TILE):
                where = (pl.ds(h * R + i * TILE, TILE), pl.ds(q * CW, CW))
                value = acc[where]
                value = value * value * kbuf[h, i : i + 1, pl.ds(q * CW, CW)]
                acc[where] = value
                total = total + jnp.sum(value, axis=0, keepdims=True)
        tsend[q] = jnp.broadcast_to(total, (8, CW))
        for d in range(1, nz):
            to = dev(x, y, lax.rem(z + d, nz), c)
            go(remote(tsend.at[q], trecv.at[z, q], t_send.at[d, q], t_recv.at[z, q], to))

    def finish(q):
        total = tsend[q]
        for d in range(1, nz):
            zb = lax.rem(z + d, nz)
            remote(tsend.at[q], trecv.at[zb, q], t_send.at[d, q], t_recv.at[zb, q], partner).wait_recv()
            total = total + trecv[zb, q]
        scale = (order / total)[0:1, :]
        for h in range(2):
            for i in range(R // TILE):
                where = (pl.ds(h * R + i * TILE, TILE), pl.ds(q * CW, CW))
                obuf[where] = (acc[where] * scale).astype(jnp.bfloat16)
        for h in range(2):
            src = obuf.at[pl.ds(h * R, R), pl.ds(q * CW, CW)]
            dst = out.at[:, cols(c * H + q * CW, CW)]
            here = jnp.logical_and(home, y == h)
            go(remote(src, dst, o_send.at[h, q], o_recv.at[c, q], dev(x, h, z, y)), jnp.logical_not(here))

            @pl.when(here)
            def _():
                pltpu.make_async_copy(src, dst, o_recv.at[c, q]).start()

    def panel_ready():
        pa_arrive(1)
        pl.when(home)(functools.partial(pa_arrive, 0))
        for q in range(nq):
            y_passed(q, 1)
        ref = rp.at[rows(oy), cols((2 * x + oc) * W, W)]
        pl.when(home)(remote(ref, ref, yb_send.at[1], yb_recv.at[1], partner).wait_recv)
        x_passed(xf_recv, xf_send, y)
        x_passed(xg_recv, xg_send, oy)
        for h in range(2):
            pltpu.make_async_copy(kbuf.at[h], kbuf.at[h], k_recv.at[h]).wait()

    steps = nq + nz - 2
    done, ahead = 0, None
    for s in range(max(steps, 4)):
        if s < nq:
            if s == 0:
                pl.when(jnp.logical_not(home))(functools.partial(pa_arrive, 0))
            own_sends(s, 0)
            if s == 0:
                y_pieces(0)
            if s == 1:
                for q in range(1, nq):
                    y_pieces(q)
                pass_x(home)
                go(remote(mine, mine, yb_send.at[0], yb_recv.at[0], across), home)
            y_passed(s, 0)
            own_sends(s, 1)
        if s == 2:
            pl.when(jnp.logical_not(home))(
                remote(ycol_ref, ycol_ref, yb_send.at[0], yb_recv.at[0], across).wait_recv
            )
            go(remote(ycol_ref, ycol_ref, yb_send.at[1], yb_recv.at[1], partner), jnp.logical_not(home))
            pass_x(jnp.logical_not(home))
        for d in range(1, nz):
            q = s + 1 - d
            if 0 <= q < nq:
                arrivals(d, q, True)
                arrivals(d, q, False)
        if s == 2:
            x_arrive(xo_recv, xo_send, xf_recv, xf_send, y)
        if s == 3:
            x_arrive(xd_recv, xd_send, xg_recv, xg_send, oy)
            panel_ready()
        ready = [q for q in range(done, nq) if s >= max(q + nz - 2, 3)]
        for q in ready:
            multiply(q, list(range(nz - 1 if q == ahead else 0, nz)))
            inflate(q)
        for q in ready:
            finish(q)
        done += len(ready)
        if s >= 3 and s == nq + nz - 4 and done == nq - 1:
            ahead = done
            multiply(ahead, list(range(nz - 1)))
    for hh in range(2):
        for q in range(nq):
            ref = out.at[:, pl.ds(hh * H + q * CW, CW)]
            pltpu.make_async_copy(ref, ref, o_recv.at[hh, q]).wait()
    for copy, cond in started:
        if cond is None:
            copy.wait_send()
        else:
            pl.when(cond)(copy.wait_send)


def body(similarity, occupancy, kept_tiles):
    R, W = similarity.shape
    nrow, ncol = lax.axis_size("row"), lax.axis_size("col")
    nz, nx = nrow // 2, ncol // 2
    H = W // 2
    nq = H // TILE
    CW = H // nq
    order = R * nrow
    kept_rows = -(-(R // TILE) // 8) * 8
    dma = pltpu.SemaphoreType.DMA
    vmem = pltpu.VMEM
    return pl.pallas_call(
        functools.partial(kernel, nz, nx, nq, float(order)),
        out_shape=jax.ShapeDtypeStruct((R, W), jnp.bfloat16),
        in_specs=[
            pl.BlockSpec(memory_space=pltpu.VMEM),
            pl.BlockSpec(memory_space=pltpu.SMEM),
            pl.BlockSpec(memory_space=pltpu.SMEM),
        ],
        out_specs=pl.BlockSpec(memory_space=pltpu.VMEM),
        scratch_shapes=[
            vmem((2 * R, order), jnp.bfloat16),
            vmem((nz, 2 * R, H), jnp.bfloat16),
            vmem((2 * R, H), jnp.float32),
            vmem((2 * R, H), jnp.bfloat16),
            vmem((nq, 8, CW), jnp.float32),
            vmem((nz, nq, 8, CW), jnp.float32),
            vmem((kept_rows, W), jnp.float32),
            vmem((2, kept_rows, H), jnp.float32),
            dma((2, nz, nq, 2)), dma((nz, nq, 2)),
            dma((2,)), dma((2,)),
            dma((nq, 2)), dma((nq, 2)),
            dma((nq, 2)), dma((nq, 2)),
            dma((2,)), dma((2,)),
            dma((nx,)), dma((nx,)),
            dma((nx,)), dma((nx,)),
            dma((nx,)), dma((nx,)),
            dma((nx,)), dma((nx,)),
            dma((nz, nq)), dma((nz, nq)),
            dma((2, nq)), dma((2, nq)),
            dma((2,)), dma((2,)),
        ],
        compiler_params=pltpu.CompilerParams(
            collective_id=0, has_side_effects=True, vmem_limit_bytes=48 * 2**20
        ),
    )(similarity, occupancy, kept_tiles)


def solution(mesh):
    placed = (P("row", "col"), P("row", "col"), P("row", "col"))
    return jax.shard_map(
        body, mesh=mesh, in_specs=placed, out_specs=P("row", "col"), check_vma=False
    )
```

```python
import functools

import jax
import jax.numpy as jnp
from jax import lax
from jax.experimental import pallas as pl
from jax.experimental.pallas import tpu as pltpu
from jax.sharding import PartitionSpec as P

TILE = 128
MESH = pl.DeviceIdType.MESH


def kernel(
    nz, nx, nq, order,
    sim_any, occ_any, kept_any, out,
    sim, occ, kept, rp, cp, acc, obuf, tsend, trecv, ksend, kbuf,
    z_send, z_recv, pa_send, pa_recv, yc_send, yc_recv, yf_send, yf_recv,
    yb_send, yb_recv, xo_send, xo_recv, xf_send, xf_recv, xd_send, xd_recv, xg_send, xg_recv,
    t_send, t_recv, o_send, o_recv, k_send, k_recv, in_sem,
):
    R, W = sim.shape
    H = W // 2
    CW = H // nq
    ir, ic = lax.axis_index("row"), lax.axis_index("col")
    z, y = lax.div(ir, 2), lax.rem(ir, 2)
    x, c = lax.div(ic, 2), lax.rem(ic, 2)
    oy, oc = 1 - y, 1 - c
    home = c == y

    def dev(xx, yy, zz, cc):
        return (zz * 2 + yy, xx * 2 + cc)

    def mult(v, m):
        return pl.multiple_of(v, m)

    def rows(yy):
        return pl.ds(mult(yy * R, R), R)

    def cols(start, width):
        return pl.ds(mult(start, TILE), width)

    def remote(src, dst, ssem, rsem, to):
        return pltpu.make_async_remote_copy(
            src_ref=src, dst_ref=dst, send_sem=ssem, recv_sem=rsem, device_id=to, device_id_type=MESH
        )

    partner = dev(x, y, z, oc)
    across = dev(x, oy, z, c)
    started = []

    def go(copy, cond=None):
        if cond is None:
            copy.start()
        else:
            pl.when(cond)(copy.start)
        started.append((copy, cond))

    barrier = pltpu.get_barrier_semaphore()
    peers = [partner, across, dev(x, oy, z, oc)]
    peers += [dev(lax.rem(x + d, nx), y, z, c) for d in range(1, nx)]
    peers += [dev(x, y, lax.rem(z + d, nz), c) for d in range(1, nz)]
    for peer in peers:
        pl.semaphore_signal(barrier, inc=1, device_id=peer, device_id_type=MESH)

    loads = [
        pltpu.make_async_copy(src, dst, in_sem.at[i])
        for i, (src, dst) in enumerate(((sim_any, sim), (occ_any, occ), (kept_any, kept)))
    ]
    for load in loads:
        load.start()
    for load in loads:
        load.wait()

    mycol = (2 * x + c) * W
    for i in range(R // TILE):
        for j in range(W // TILE):
            flag = occ[i : i + 1, j : j + 1].astype(jnp.float32)
            tile = sim[i * TILE : (i + 1) * TILE, j * TILE : (j + 1) * TILE].astype(jnp.float32)
            rp[pl.ds(mult(y * R + i * TILE, TILE), TILE), cols(mycol + j * TILE, TILE)] = (tile * flag).astype(
                jnp.bfloat16
            )
    ksend[...] = jnp.zeros_like(ksend)
    for i in range(R // TILE):
        for j in range(W // TILE):
            ksend[i : i + 1, j * TILE : (j + 1) * TILE] = jnp.broadcast_to(
                kept[i : i + 1, j : j + 1].astype(jnp.float32), (1, TILE)
            )
    pl.semaphore_wait(barrier, len(peers))

    mine = rp.at[rows(y), cols(mycol, W)]

    def half_of(yy, start, hh):
        return rp.at[rows(yy), cols(start + hh * H, H)]

    for j, hh in enumerate((oc, c)):
        ref = half_of(y, mycol, hh)
        go(remote(ref, ref, pa_send.at[j], pa_recv.at[j], partner))

    def pa_arrive(j):
        ref = half_of(y, (2 * x + oc) * W, c if j == 0 else oc)
        remote(ref, ref, pa_send.at[j], pa_recv.at[j], partner).wait_recv()

    def piece(yy, core, q, hh):
        return rp.at[rows(yy), cols((2 * x + core) * W + hh * H + q * CW, CW)]

    for q in range(nq):
        for j, hh in enumerate((oc, c)):
            ref = piece(y, c, q, hh)
            go(remote(ref, ref, yc_send.at[q, j], yc_recv.at[q, j], across), jnp.logical_not(home))

    for d in range(1, nx):
        to = dev(lax.rem(x + d, nx), y, z, c)
        go(remote(mine, mine, xo_send.at[d], xo_recv.at[d], to))

    for hh in range(2):
        src = ksend.at[:, pl.ds(hh * H, H)]
        here = jnp.logical_and(home, c == hh)
        go(
            remote(src, kbuf.at[y], k_send.at[hh], k_recv.at[y], dev(x, c, z, hh)),
            jnp.logical_not(here),
        )

        @pl.when(here)
        def _():
            pltpu.make_async_copy(src, kbuf.at[y], k_recv.at[y]).start()

    tcol = (2 * x + y) * W + c * H

    def yy_of(h):
        return y if h == 0 else oy

    def own_part(q, h):
        return rp.at[rows(yy_of(h)), cols(tcol + q * CW, CW)]

    def slot(zb, q, h):
        return cp.at[zb, rows(yy_of(h)), pl.ds(q * CW, CW)]

    def own_sends(q, h):
        go(
            remote(own_part(q, h), slot(z, q, h), z_send.at[0, z, q, h], z_recv.at[z, q, h], dev(x, y, lax.rem(z + 1, nz), c)),
            z < nz - 1,
        )
        go(
            remote(own_part(q, h), slot(z, q, h), z_send.at[1, z, q, h], z_recv.at[z, q, h], dev(x, y, lax.rem(z + nz - 1, nz), c)),
            z > 0,
        )

    def arrivals(d, q, up):
        zb = lax.rem(z + nz - d, nz) if up else lax.rem(z + d, nz)
        valid = z >= d if up else z + d < nz
        onward = jnp.logical_and(valid, z < nz - 1) if up else jnp.logical_and(valid, z > 0)
        nxt = lax.rem(z + 1, nz) if up else lax.rem(z + nz - 1, nz)
        side = 0 if up else 1
        for h in range(2):
            ref = slot(zb, q, h)
            copy = remote(ref, ref, z_send.at[side, zb, q, h], z_recv.at[zb, q, h], dev(x, y, nxt, c))
            pl.when(valid)(copy.wait_recv)
            go(copy, onward)

    def y_pieces(q):
        for j, hh in enumerate((oc, c)):
            ref = piece(oy, c, q, hh)
            pl.when(home)(remote(ref, ref, yc_send.at[q, j], yc_recv.at[q, j], across).wait_recv)
            go(remote(ref, ref, yf_send.at[q, j], yf_recv.at[q, j], partner), home)

    def y_passed(q, j):
        ref = piece(oy, oc, q, c if j == 0 else oc)
        pl.when(jnp.logical_not(home))(
            remote(ref, ref, yf_send.at[q, j], yf_recv.at[q, j], partner).wait_recv
        )

    ycol_ref = rp.at[rows(oy), cols(mycol, W)]

    def pass_x(cond):
        for d in range(1, nx):
            to = dev(lax.rem(x + d, nx), y, z, c)
            go(remote(ycol_ref, ycol_ref, xd_send.at[d], xd_recv.at[d], to), cond)

    def x_arrive(recv, send, recv2, send2, yy):
        for d in range(1, nx):
            src_x = lax.rem(x + nx - d, nx)
            ref = rp.at[rows(yy), cols((2 * src_x + c) * W, W)]
            remote(ref, ref, send.at[d], recv.at[d], partner).wait_recv()
            go(remote(ref, ref, send2.at[d], recv2.at[d], partner))

    def x_passed(recv2, send2, yy):
        for d in range(1, nx):
            src_x = lax.rem(x + nx - d, nx)
            ref = rp.at[rows(yy), cols((2 * src_x + oc) * W, W)]
            remote(ref, ref, send2.at[d], recv2.at[d], partner).wait_recv()

    low = z < (nz + 1) // 2

    def zb_of(d):
        return jnp.where(low, lax.rem(z + d, nz), lax.rem(z + nz - d, nz))

    def multiply(q, ds):
        for h in range(2):
            part = None
            for d in ds:
                zb = zb_of(d) if d else z
                lhs = rp[pl.ds(h * R, R), pl.ds(mult(zb * 2 * R, 2 * R), 2 * R)]
                if d:
                    rhs = cp[zb, :, pl.ds(q * CW, CW)]
                else:
                    rhs = rp[:, cols(tcol + q * CW, CW)]
                prod = jnp.dot(lhs, rhs, preferred_element_type=jnp.float32)
                part = prod if part is None else part + prod
            where = (pl.ds(h * R, R), pl.ds(q * CW, CW))
            if ds[0]:
                acc[where] = acc[where] + part
            else:
                acc[where] = part

    def inflate(q):
        total = jnp.zeros((1, CW), jnp.float32)
        for h in range(2):
            for i in range(R // TILE):
                where = (pl.ds(h * R + i * TILE, TILE), pl.ds(q * CW, CW))
                value = acc[where]
                value = value * value * kbuf[h, i : i + 1, pl.ds(q * CW, CW)]
                acc[where] = value
                total = total + jnp.sum(value, axis=0, keepdims=True)
        tsend[q] = jnp.broadcast_to(total, (8, CW))
        for d in range(1, nz):
            to = dev(x, y, lax.rem(z + d, nz), c)
            go(remote(tsend.at[q], trecv.at[z, q], t_send.at[d, q], t_recv.at[z, q], to))

    def finish(q):
        total = tsend[q]
        for d in range(1, nz):
            zb = lax.rem(z + d, nz)
            remote(tsend.at[q], trecv.at[zb, q], t_send.at[d, q], t_recv.at[zb, q], partner).wait_recv()
            total = total + trecv[zb, q]
        scale = (order / total)[0:1, :]
        for h in range(2):
            for i in range(R // TILE):
                where = (pl.ds(h * R + i * TILE, TILE), pl.ds(q * CW, CW))
                obuf[where] = (acc[where] * scale).astype(jnp.bfloat16)
        for h in range(2):
            src = obuf.at[pl.ds(h * R, R), pl.ds(q * CW, CW)]
            dst = out.at[:, cols(c * H + q * CW, CW)]
            here = jnp.logical_and(home, y == h)
            go(remote(src, dst, o_send.at[h, q], o_recv.at[c, q], dev(x, h, z, y)), jnp.logical_not(here))

            @pl.when(here)
            def _():
                pltpu.make_async_copy(src, dst, o_recv.at[c, q]).start()

    def panel_ready():
        pa_arrive(1)
        pl.when(home)(functools.partial(pa_arrive, 0))
        for q in range(nq):
            y_passed(q, 1)
        ref = rp.at[rows(oy), cols((2 * x + oc) * W, W)]
        pl.when(home)(remote(ref, ref, yb_send.at[1], yb_recv.at[1], partner).wait_recv)
        x_passed(xf_recv, xf_send, y)
        x_passed(xg_recv, xg_send, oy)
        for h in range(2):
            pltpu.make_async_copy(kbuf.at[h], kbuf.at[h], k_recv.at[h]).wait()

    pl.when(jnp.logical_not(home))(functools.partial(pa_arrive, 0))
    for q in range(nq):
        own_sends(q, 0)
    for q in range(nq):
        y_pieces(q)
        y_passed(q, 0)
        own_sends(q, 1)
    pass_x(home)
    go(remote(mine, mine, yb_send.at[0], yb_recv.at[0], across), home)
    for d in range(1, nz - 1):
        for q in range(nq):
            arrivals(d, q, True)
            arrivals(d, q, False)
        if d == 1:
            pl.when(jnp.logical_not(home))(
                remote(ycol_ref, ycol_ref, yb_send.at[0], yb_recv.at[0], across).wait_recv
            )
            go(remote(ycol_ref, ycol_ref, yb_send.at[1], yb_recv.at[1], partner), jnp.logical_not(home))
            pass_x(jnp.logical_not(home))
            x_arrive(xo_recv, xo_send, xf_recv, xf_send, y)
    x_arrive(xd_recv, xd_send, xg_recv, xg_send, oy)
    panel_ready()
    for q in range(nq):
        multiply(q, list(range(nz - 1)))
    for q in range(nq):
        arrivals(nz - 1, q, True)
        arrivals(nz - 1, q, False)
        multiply(q, [nz - 1])
        inflate(q)
        if q:
            finish(q - 1)
    finish(nq - 1)
    for hh in range(2):
        for q in range(nq):
            ref = out.at[:, pl.ds(hh * H + q * CW, CW)]
            pltpu.make_async_copy(ref, ref, o_recv.at[hh, q]).wait()
    for copy, cond in started:
        if cond is None:
            copy.wait_send()
        else:
            pl.when(cond)(copy.wait_send)


def body(similarity, occupancy, kept_tiles):
    R, W = similarity.shape
    nrow, ncol = lax.axis_size("row"), lax.axis_size("col")
    nz, nx = nrow // 2, ncol // 2
    H = W // 2
    nq = H // TILE
    CW = H // nq
    order = R * nrow
    kept_rows = -(-(R // TILE) // 8) * 8
    dma = pltpu.SemaphoreType.DMA
    vmem = pltpu.VMEM
    return pl.pallas_call(
        functools.partial(kernel, nz, nx, nq, float(order)),
        out_shape=jax.ShapeDtypeStruct((R, W), jnp.bfloat16),
        in_specs=[pl.BlockSpec(memory_space=pltpu.HBM)] * 3,
        out_specs=pl.BlockSpec(memory_space=pltpu.HBM),
        scratch_shapes=[
            vmem((R, W), jnp.bfloat16),
            vmem(occupancy.shape, jnp.int32),
            vmem(kept_tiles.shape, jnp.int32),
            vmem((2 * R, order), jnp.bfloat16),
            vmem((nz, 2 * R, H), jnp.bfloat16),
            vmem((2 * R, H), jnp.float32),
            vmem((2 * R, H), jnp.bfloat16),
            vmem((nq, 8, CW), jnp.float32),
            vmem((nz, nq, 8, CW), jnp.float32),
            vmem((kept_rows, W), jnp.float32),
            vmem((2, kept_rows, H), jnp.float32),
            dma((2, nz, nq, 2)), dma((nz, nq, 2)),
            dma((2,)), dma((2,)),
            dma((nq, 2)), dma((nq, 2)),
            dma((nq, 2)), dma((nq, 2)),
            dma((2,)), dma((2,)),
            dma((nx,)), dma((nx,)),
            dma((nx,)), dma((nx,)),
            dma((nx,)), dma((nx,)),
            dma((nx,)), dma((nx,)),
            dma((nz, nq)), dma((nz, nq)),
            dma((2, nq)), dma((2, nq)),
            dma((2,)), dma((2,)),
            dma((3,)),
        ],
        compiler_params=pltpu.CompilerParams(
            collective_id=0, has_side_effects=True, vmem_limit_bytes=63 * 2**20
        ),
    )(similarity, occupancy, kept_tiles)


def solution(mesh):
    placed = (P("row", "col"), P("row", "col"), P("row", "col"))
    return jax.shard_map(
        body, mesh=mesh, in_specs=placed, out_specs=P("row", "col"), check_vma=False
    )
```
